32 devices in a mesh: grp: 2 (over x), pre: 2 (over core), head: 8 (over z, y).
Axes of the slice: x: 2, y: 2, z: 4, core: 2. Of those that a mesh axis runs over, the one named last changes fastest.
Arguments:
- hidden: bfloat16 [1024, 14336], P(('grp', 'pre'), 'head'), parts along dimension 0, may hold values from -6 to 6
- slot_tokens: int32 [1024], P('grp'), parts along dimension 0, may hold values from 0 to 511, each once
- lengths: int32 [4, 16], P(('grp', 'pre')), parts along dimension 0, may hold values from 1 to 64, 256 in all within a row
- decode_rows: bfloat16 [64, 4, 14336], P('grp', None, 'pre'), parts along dimension 0, may hold values from -52 to 52
- query_weight: bfloat16 [14336, 2048], P('pre', 'head'), may hold values from -0.046875 to 0.046875
- key_weight: bfloat16 [14336, 2048], P('pre', 'head'), may hold values from -0.046875 to 0.046875
- value_weight: bfloat16 [14336, 2048], P('pre', 'head'), may hold values from -0.046875 to 0.046875
Outputs:
- attended: bfloat16 [64, 4, 2048], P(('grp', 'pre'), None, 'head'), parts along dimension 0
The draws below stay inside these ranges and needn't reach their ends.
There are 2 independent parts, one for each index of `grp`. The reference program is written for one: setup_inputs(seed, part) draws one part's arguments, and reference() takes and returns one part's arrays. A program takes and returns all parts, laid end to end along the dimension named above; an argument that names none is the same for every part. Nothing has to cross between parts.
Inputs may be any that keep to these rules, and one draw needn't show every extreme that they name: `slot_tokens`: each prompt token stands in exactly one cache slot. The lengths of one owner's requests add up to 256; in each row the longest is 64.
All inputs are finite; a program needn't handle non-finite values.
Results may differ from the reference program's by a relative error of at most 0.012.
The reference program's roundings to bfloat16 on the way (of `weights`) count: a program that leaves them out, or rounds other values in their place, can miss the bound.
Values may be sent and summed in bfloat16 or wider, within the bound.
No kernel may reach another device: no remote copies, remote signals or barrier semaphores. Data moves between devices by JAX's collectives and lax.ppermute only.
A program may use at most 128 MiB of HBM per device.

```python
import math
import jax
import jax.numpy as jnp
import numpy as np

D = 14336
HS = 128
STEPS = 4
PRE_TOK = 256
RH = 16
HEADS = 16
TOK = 512
REQ = 32
N_PRE = 2


def draw_decode_rows(key, part):
    key = jax.random.fold_in(key, 11)
    base = jax.random.truncated_normal(key, -6.0, 6.0, (REQ, STEPS, D), jnp.float32)
    return base.astype(jnp.bfloat16)


def level_of(rng, shape, shards, smallest, top_value):
    level, own = 1.0, jax.random.fold_in(rng, 6)
    for position, parts in shards:
        steps = jnp.exp(jax.random.uniform(jax.random.fold_in(own, position), (parts,), jnp.float32, smallest / len(shards), top_value / len(shards)))
        level = level * jnp.repeat(steps, shape[position] // parts).reshape([-1 if axis == position else 1 for axis in range(len(shape))])
    return level


def split_up(count, total, reach, skew):
    weights = [(1 << 20) // math.isqrt(rank ** skew) + 1 for rank in range(2, count + 1)]
    spare, holding = total - reach - (count - 1), [1] * (count - 1)
    while spare > 0:
        free = [i for i in range(count - 1) if holding[i] < reach]
        whole, remaining = sum([weights[i] for i in free]), spare
        for i in free:
            extra = min(reach - holding[i], max(1, remaining * weights[i] // whole), spare)
            holding[i] = holding[i] + extra
            spare = spare - extra
    return np.array([reach] + holding)


def uneven_parts(stream_key, number_of, total, most, skew):
    if number_of == 2:
        one = jax.random.randint(stream_key, (), max(1, total - most), min(most, total - 1) + 1)
        return jnp.stack([one, total - one])
    sizes = jnp.asarray(split_up(number_of, total, most, skew), jnp.int32)
    twos = (number_of - 1) // 2
    donor, sink = sizes[1:1 + 2 * twos:2], sizes[2:2 + 2 * twos:2]
    margin = jnp.minimum(donor - 1, most - sink)
    shifted = jax.random.randint(jax.random.fold_in(stream_key, 1), (twos,), 0, 1 << 20) % (margin + 1)
    sizes = sizes.at[1:1 + 2 * twos:2].set(donor - shifted).at[2:2 + 2 * twos:2].set(sink + shifted)
    return sizes[jax.random.permutation(jax.random.fold_in(stream_key, 2), number_of)]


def scatter_about(key, extent, scale, reach, cuts=(), held_as=jnp.bfloat16):
    gain = level_of(key, extent, cuts, -0.22, 0.18) if cuts else 1.0
    drawn = jax.random.normal(key, extent, jnp.float32) * scale * gain
    return jnp.minimum(jnp.maximum(drawn, -reach), reach).astype(held_as)


def setup_inputs(seed: int = 0, part: int = 0) -> dict:
    splits = jax.random.split(jax.random.key(seed), 8)
    part_splits = jax.random.split(jax.random.fold_in(splits[7], part), 8)
    hidden = scatter_about(part_splits[0], (TOK, D), 1.0, 6.0, ((0, 2), (1, 8)))
    slot_tokens = jax.random.permutation(part_splits[1], TOK).astype(jnp.int32)
    lengths = jax.vmap(lambda own: uneven_parts(own, RH, PRE_TOK, PRE_TOK // 4, 2))(jax.random.split(part_splits[2], N_PRE)).reshape((N_PRE, RH)).astype(jnp.int32)
    decode_rows = draw_decode_rows(jax.random.fold_in(jax.random.fold_in(splits[7], part), 71), part)
    query_weight = scatter_about(splits[4], (D, HEADS * HS), D ** -0.5, 0.046875, ((0, 2), (1, 8)))
    key_weight = scatter_about(splits[5], (D, HEADS * HS), D ** -0.5, 0.046875, ((0, 2), (1, 8)))
    value_weight = scatter_about(splits[6], (D, HEADS * HS), D ** -0.5, 0.046875, ((0, 2), (1, 8)))
    return dict(hidden=hidden, slot_tokens=slot_tokens, lengths=lengths, decode_rows=decode_rows, query_weight=query_weight, key_weight=key_weight, value_weight=value_weight)


def reference(hidden, slot_tokens, lengths, decode_rows, query_weight, key_weight, value_weight):
    keys = jnp.dot(hidden, key_weight, preferred_element_type=jnp.float32).astype(jnp.bfloat16)
    values = jnp.dot(hidden, value_weight, preferred_element_type=jnp.float32).astype(jnp.bfloat16)
    key_cache = keys[slot_tokens].reshape(TOK, HEADS, HS).astype(jnp.float32)
    value_cache = values[slot_tokens].reshape(TOK, HEADS, HS).astype(jnp.float32)
    flat = decode_rows.reshape(REQ * STEPS, D)
    new_query = jnp.dot(flat, query_weight, preferred_element_type=jnp.float32).astype(jnp.bfloat16)
    new_key = jnp.dot(flat, key_weight, preferred_element_type=jnp.float32).astype(jnp.bfloat16)
    new_value = jnp.dot(flat, value_weight, preferred_element_type=jnp.float32).astype(jnp.bfloat16)
    query = new_query.reshape(REQ, STEPS, HEADS, HS).astype(jnp.float32)
    fresh_key = new_key.reshape(REQ, STEPS, HEADS, HS).astype(jnp.float32)
    fresh_value = new_value.reshape(REQ, STEPS, HEADS, HS).astype(jnp.float32)
    within = jnp.cumsum(lengths, axis=1) - lengths
    starts = (within + jnp.arange(N_PRE, dtype=jnp.int32)[:, None] * PRE_TOK).reshape(-1)
    lens = lengths.reshape(-1)
    heads_index = jnp.arange(HEADS).astype(jnp.float32)
    slope = jnp.exp2(-8.0 * (heads_index + 1.0) / HEADS)
    scale = 1.0 / (HS ** 0.5)
    step_index = jnp.arange(STEPS, dtype=jnp.int32)
    slot_index = jnp.arange(TOK, dtype=jnp.int32)
    rel = slot_index[None, :] - starts[:, None]
    valid = (rel >= 0) & (rel < lens[:, None])
    dist = (lens[:, None, None] + step_index[None, :, None] - rel[:, None, :]).astype(jnp.float32)
    ctx = jnp.einsum("rshd,jhd->rshj", query, key_cache) * scale
    ctx = ctx - slope[None, None, :, None] * dist[:, :, None, :]
    ctx = jnp.where(valid[:, None, None, :], ctx, -1e30)
    near = jnp.einsum("rshd,rthd->rsht", query, fresh_key) * scale
    tdist = (step_index[:, None] - step_index[None, :]).astype(jnp.float32)
    near = near - slope[None, None, :, None] * tdist[None, :, None, :]
    near = jnp.where((step_index[None, :] <= step_index[:, None])[None, :, None, :], near, -1e30)
    top = jnp.maximum(jnp.max(ctx, axis=-1), jnp.max(near, axis=-1))
    part_ctx = jnp.exp(ctx - top[..., None])
    part_near = jnp.exp(near - top[..., None])
    total = jnp.sum(part_ctx, axis=-1) + jnp.sum(part_near, axis=-1)
    weight_ctx = (part_ctx / total[..., None]).astype(jnp.bfloat16).astype(jnp.float32)
    weight_near = (part_near / total[..., None]).astype(jnp.bfloat16).astype(jnp.float32)
    out = jnp.einsum("rshj,jhd->rshd", weight_ctx, value_cache) + jnp.einsum("rsht,rthd->rshd", weight_near, fresh_value)
    return out.reshape(REQ, STEPS, HEADS * HS).astype(jnp.bfloat16)
```

```python
import functools

import jax
import jax.numpy as jnp
import numpy as np
from jax import lax
from jax.experimental import pallas as pl
from jax.experimental.pallas import tpu as pltpu
from jax.sharding import PartitionSpec as P

HS = 128


def ring_order(n):
    if n == 8:
        return [0, 2, 4, 6, 7, 5, 3, 1]
    return list(range(n))


def step_kernel(count, first, rows_ref, *refs):
    items = refs[:count]
    acc_ref, wk, wv, wk_far, wv_far = refs[count : count + 5]
    out_ref, held, sems = refs[count + 5 :]
    depth = held.shape[1]
    cols = wk.shape[1]

    def copies(i, keys, values):
        start = pl.multiple_of(rows_ref[2 * (first + i)], 32)
        return [
            pltpu.make_async_copy(
                src.at[pl.ds(start, depth), :], held.at[i, :, pl.ds(part * cols, cols)], sems.at[i, part]
            )
            for part, src in enumerate((keys, values))
        ]

    for i in range(count):

        @pl.when(rows_ref[2 * (first + i) + 1] == 0)
        def _():
            for copy in copies(i, wk, wv):
                copy.start()

        @pl.when(rows_ref[2 * (first + i) + 1] != 0)
        def _():
            for copy in copies(i, wk_far, wv_far):
                copy.start()

    total = acc_ref[...]
    for i in range(count):
        for copy in copies(i, wk, wv):
            copy.wait()
        term = jnp.dot(items[i][...], held[i], preferred_element_type=jnp.float32)
        total = total + term
    out_ref[...] = total.astype(out_ref.dtype)


def step(items, acc, rows, first, weights, dtype=jnp.float32):
    count = len(items)
    tok, depth = items[0].shape
    cols = weights[0].shape[1]
    vmem = pl.BlockSpec(memory_space=pltpu.VMEM)
    return pl.pallas_call(
        functools.partial(step_kernel, count, first),
        out_shape=jax.ShapeDtypeStruct((tok, 2 * cols), dtype),
        in_specs=[pl.BlockSpec(memory_space=pltpu.SMEM)]
        + [vmem] * (count + 1)
        + [pl.BlockSpec(memory_space=pl.ANY)] * 4,
        out_specs=vmem,
        scratch_shapes=[
            pltpu.VMEM((count, depth, 2 * cols), jnp.bfloat16),
            pltpu.SemaphoreType.DMA((count, 2)),
        ],
        compiler_params=pltpu.CompilerParams(vmem_limit_bytes=24 * 1024 * 1024),
        cost_estimate=pl.CostEstimate(
            flops=2 * count * tok * depth * 2 * cols,
            bytes_accessed=count * (tok * depth * 2 + depth * cols * 4) + tok * cols * 16,
            transcendentals=0,
        ),
    )(rows, *items, acc, *weights)


def attend_kernel(steps, slope_ref, fresh_ref, own_ref, far_ref, place_ref, span_ref, out_ref):
    rows = fresh_ref.shape[0]
    cols = fresh_ref.shape[1] // 3
    tok = own_ref.shape[0]
    scale = 1.0 / HS**0.5
    start = span_ref[:, 0:1]
    length = span_ref[:, 1:2]
    row = lax.broadcasted_iota(jnp.int32, (rows, 1), 0)
    step_of = row % steps
    rel = place_ref[...] - start
    valid = (rel >= 0) & (rel < length)
    dist = (length + step_of - rel).astype(jnp.float32)
    col = lax.broadcasted_iota(jnp.int32, (1, rows), 1)
    near_ok = (row // steps == col // steps) & (col <= row)
    near_dist = (row - col).astype(jnp.float32)
    nt = (((1,), (1,)), ((), ()))
    for head in range(cols // HS):
        slope = slope_ref[head]
        query = fresh_ref[:, head * HS : (head + 1) * HS]
        fresh_key = fresh_ref[:, cols + head * HS : cols + (head + 1) * HS]
        fresh_value = fresh_ref[:, 2 * cols + head * HS : 2 * cols + (head + 1) * HS]
        scores = []
        for part, ref in enumerate((own_ref, far_ref)):
            key = ref[:, head * HS : (head + 1) * HS]
            ctx = lax.dot_general(query, key, nt, preferred_element_type=jnp.float32) * scale
            ctx = ctx - slope * dist[:, part * tok : (part + 1) * tok]
            scores.append(jnp.where(valid[:, part * tok : (part + 1) * tok], ctx, -1e30))
        near = lax.dot_general(query, fresh_key, nt, preferred_element_type=jnp.float32) * scale
        scores.append(jnp.where(near_ok, near - slope * near_dist, -1e30))
        top = functools.reduce(jnp.maximum, [jnp.max(s, axis=1, keepdims=True) for s in scores])
        exps = [jnp.exp(s - top) for s in scores]
        total = sum(jnp.sum(e, axis=1, keepdims=True) for e in exps)
        weights = [(e / total).astype(jnp.bfloat16) for e in exps]
        values = [ref[:, cols + head * HS : cols + (head + 1) * HS] for ref in (own_ref, far_ref)]
        values.append(fresh_value)
        out = sum(
            jnp.dot(w, v, preferred_element_type=jnp.float32) for w, v in zip(weights, values)
        )
        out_ref[:, head * HS : (head + 1) * HS] = out.astype(out_ref.dtype)


def on_device(hidden, slot_tokens, lengths, decode_rows, query_weight, key_weight, value_weight):
    group = lax.axis_index("head")
    owner = lax.axis_index("pre")
    n = lax.axis_size("head")
    own_tok, width = hidden.shape
    depth = key_weight.shape[0]
    cols = key_weight.shape[1]
    heads_dev = cols // HS
    swap = [(0, 1), (1, 0)]

    order = ring_order(n)
    up = [(order[i], order[(i + 1) % n]) for i in range(n)]
    down = [(order[i], order[(i - 1) % n]) for i in range(n)]
    place = [0] * n
    for i, g in enumerate(order):
        place[g] = i
    half = width // 2

    own = [hidden[:, :half], hidden[:, half:]]
    ups, downs = list(own), list(own)
    arrivals = []
    for s in range(1, n // 2 + 1):
        last = s == n // 2
        for i in range(2):
            if not last or i == 0:
                ups[i] = lax.ppermute(ups[i], "head", up)
                downs[1 - i] = lax.ppermute(downs[1 - i], "head", down)
                arrivals.append(((ups[i], -s, i), (downs[1 - i], s, 1 - i)))

    seen = [(0, 0), (0, 1)] + [(d, part) for pair in arrivals for _, d, part in pair]
    table = np.zeros((2 * n, 2 * len(seen)), np.int32)
    for g in range(n):
        for k, (distance, part) in enumerate(seen):
            row = order[(place[g] + distance) % n] * width + part * half
            for p in range(2):
                table[2 * g + p, 2 * k : 2 * k + 2] = row % depth, row // depth != p
    rows_of = lax.dynamic_slice_in_dim(jnp.asarray(table), 2 * group + owner, 1, 0)[0]

    weights = (
        key_weight,
        value_weight,
        lax.ppermute(key_weight, "pre", swap),
        lax.ppermute(value_weight, "pre", swap),
    )

    req_dev, steps = lengths.shape[1], decode_rows.shape[1]
    rows_dev = req_dev * steps
    rows = decode_rows.reshape(2 * rows_dev, depth)
    sums = jnp.concatenate(
        [jnp.dot(rows, w, preferred_element_type=jnp.float32) for w in (query_weight, key_weight, value_weight)],
        axis=1,
    )
    keep = lax.dynamic_slice_in_dim(sums, owner * rows_dev, rows_dev, 0)
    give = lax.dynamic_slice_in_dim(sums, (1 - owner) * rows_dev, rows_dev, 0)
    fresh = (keep + lax.ppermute(give, "pre", swap)).astype(jnp.bfloat16)

    mine = lax.dynamic_slice_in_dim(slot_tokens, owner * own_tok, own_tok)
    lane = jnp.arange(2 * own_tok, dtype=jnp.int32)
    token = (lane + owner * own_tok) % (2 * own_tok)
    slot = jnp.arange(1, own_tok + 1, dtype=jnp.int32)
    where = jnp.sum(jnp.where(mine[:, None] == token[None, :], slot[:, None], 0), axis=0, keepdims=True)
    lens = lengths[0]
    starts = jnp.cumsum(lens) - lens
    where = jnp.where(where == 0, -(1 << 20), where - 1)
    span = jnp.repeat(jnp.stack([starts, lens], axis=1), steps, axis=0)
    heads_index = (group * heads_dev + jnp.arange(heads_dev)).astype(jnp.float32)
    slope = jnp.exp2(-8.0 * (heads_index + 1.0) / (heads_dev * n))

    acc = step(own, jnp.zeros((own_tok, 2 * cols), jnp.float32), rows_of, 0, weights)
    for k, pair in enumerate(arrivals):
        final = k == len(arrivals) - 1
        acc = step(
            [item for item, _, _ in pair],
            acc,
            rows_of,
            2 * k + 2,
            weights,
            jnp.bfloat16 if final else jnp.float32,
        )
    far = lax.ppermute(acc, "pre", swap)
    vmem = pl.BlockSpec(memory_space=pltpu.VMEM)
    out = pl.pallas_call(
        functools.partial(attend_kernel, steps),
        out_shape=jax.ShapeDtypeStruct((rows_dev, cols), jnp.bfloat16),
        in_specs=[pl.BlockSpec(memory_space=pltpu.SMEM)] + [vmem] * 5,
        out_specs=vmem,
        compiler_params=pltpu.CompilerParams(vmem_limit_bytes=16 * 1024 * 1024),
    )(slope, fresh, acc, far, where, span)
    return out.reshape(req_dev, steps, cols)


def solution(mesh):
    in_specs = (
        P(("grp", "pre"), "head"),
        P("grp"),
        P(("grp", "pre"), None),
        P("grp", None, "pre"),
        P("pre", "head"),
        P("pre", "head"),
        P("pre", "head"),
    )
    out_specs = P(("grp", "pre"), None, "head")
    return jax.shard_map(
        on_device, mesh=mesh, in_specs=in_specs, out_specs=out_specs, check_vma=False
    )
```

```python
import functools

import jax
import jax.numpy as jnp
import numpy as np
from jax import lax
from jax.experimental import pallas as pl
from jax.experimental.pallas import tpu as pltpu
from jax.sharding import PartitionSpec as P

HS = 128


def ring_order(n):
    if n == 8:
        return [0, 2, 4, 6, 7, 5, 3, 1]
    return list(range(n))


def step_kernel(count, first, rows_ref, *refs):
    more = first >= 0
    items, refs = refs[:count], refs[count:]
    if count:
        acc_ref, now_ref, refs = refs[0], refs[1], refs[2:]
    if more:
        near, far = refs[:2], refs[2:4]
        next_ref, sems = refs[-2:]
        depth = next_ref.shape[1]
        cols = near[0].shape[1]

        def copies(i, sources):
            start = pl.multiple_of(rows_ref[2 * (first + i)], 32)
            return [
                pltpu.make_async_copy(
                    src.at[pl.ds(start, depth), :],
                    next_ref.at[i, :, pl.ds(part * cols, cols)],
                    sems.at[i, part],
                )
                for part, src in enumerate(sources)
            ]

        for i in range(2):

            @pl.when(rows_ref[2 * (first + i) + 1] == 0)
            def _():
                for copy in copies(i, near):
                    copy.start()

            @pl.when(rows_ref[2 * (first + i) + 1] != 0)
            def _():
                for copy in copies(i, far):
                    copy.start()

    if count:
        out_ref = refs[4] if more else refs[0]
        total = acc_ref[...] if acc_ref.shape[0] == items[0].shape[0] else 0.0
        for i in range(count):
            total = total + jnp.dot(items[i][...], now_ref[i], preferred_element_type=jnp.float32)
        out_ref[...] = total.astype(out_ref.dtype)
    if more:
        for i in range(2):
            for copy in copies(i, near):
                copy.wait()


def step(items, acc, now, rows, first, weights, depth, dtype=jnp.float32):
    count, more = len(items), first >= 0
    cols = 2 * weights[0].shape[1]
    vmem = pl.BlockSpec(memory_space=pltpu.VMEM)
    operands, specs = [rows, *items], [pl.BlockSpec(memory_space=pltpu.SMEM)] + [vmem] * count
    shapes = []
    if count:
        tok = items[0].shape[0]
        operands += [acc, now]
        specs += [vmem] * 2
        shapes.append(jax.ShapeDtypeStruct((tok, cols), dtype))
    if more:
        operands += weights
        specs += [pl.BlockSpec(memory_space=pl.ANY)] * 4
        shapes.append(jax.ShapeDtypeStruct((2, depth, cols), jnp.bfloat16))
    return pl.pallas_call(
        functools.partial(step_kernel, count, first),
        out_shape=shapes,
        in_specs=specs,
        out_specs=[vmem] * len(shapes),
        scratch_shapes=[pltpu.SemaphoreType.DMA((2, 2))] if more else [],
        compiler_params=pltpu.CompilerParams(vmem_limit_bytes=40 * 1024 * 1024),
        cost_estimate=pl.CostEstimate(flops=0, bytes_accessed=0, transcendentals=0),
    )(*operands)


def decode_kernel(rows_ref, wq_ref, wk_ref, wv_ref, out_ref, flat):
    count, steps, _ = rows_ref.shape
    cols = wq_ref.shape[1]
    for r in range(count):
        flat[r * steps : (r + 1) * steps] = rows_ref[r].astype(jnp.float32)
    rows = flat[...].astype(jnp.bfloat16)
    for part, ref in enumerate((wq_ref, wk_ref, wv_ref)):
        term = jnp.dot(rows, ref[...], preferred_element_type=jnp.float32)
        at = slice(part * cols, (part + 1) * cols)

        @pl.when(pl.program_id(0) == 0)
        def _():
            out_ref[:, at] = term

        @pl.when(pl.program_id(0) != 0)
        def _():
            out_ref[:, at] += term


def decode(rows, weights, block):
    count, steps, depth = rows.shape
    cols = weights[0].shape[1]
    return pl.pallas_call(
        decode_kernel,
        out_shape=jax.ShapeDtypeStruct((count * steps, 3 * cols), jnp.float32),
        grid=(depth // block,),
        in_specs=[pl.BlockSpec((count, steps, block), lambda i: (0, 0, i))]
        + [pl.BlockSpec((block, cols), lambda i: (i, 0))] * 3,
        out_specs=pl.BlockSpec((count * steps, 3 * cols), lambda i: (0, 0)),
        scratch_shapes=[pltpu.VMEM((count * steps, block), jnp.float32)],
        compiler_params=pltpu.CompilerParams(vmem_limit_bytes=56 * 1024 * 1024),
        cost_estimate=pl.CostEstimate(flops=0, bytes_accessed=0, transcendentals=0),
    )(rows, *weights)


def attend_kernel(steps, slope_ref, fresh_ref, own_ref, far_ref, place_ref, span_ref, out_ref):
    rows = fresh_ref.shape[0]
    cols = fresh_ref.shape[1] // 3
    tok = own_ref.shape[0]
    scale = 1.0 / HS**0.5
    start = span_ref[:, 0:1]
    length = span_ref[:, 1:2]
    row = lax.broadcasted_iota(jnp.int32, (rows, 1), 0)
    step_of = row % steps
    rel = place_ref[...] - start
    valid = (rel >= 0) & (rel < length)
    dist = (length + step_of - rel).astype(jnp.float32)
    col = lax.broadcasted_iota(jnp.int32, (1, rows), 1)
    near_ok = (row // steps == col // steps) & (col <= row)
    near_dist = (row - col).astype(jnp.float32)
    nt = (((1,), (1,)), ((), ()))
    for head in range(cols // HS):
        slope = slope_ref[head]
        query = fresh_ref[:, head * HS : (head + 1) * HS]
        fresh_key = fresh_ref[:, cols + head * HS : cols + (head + 1) * HS]
        fresh_value = fresh_ref[:, 2 * cols + head * HS : 2 * cols + (head + 1) * HS]
        scores = []
        for part, ref in enumerate((own_ref, far_ref)):
            key = ref[:, head * HS : (head + 1) * HS]
            ctx = lax.dot_general(query, key, nt, preferred_element_type=jnp.float32) * scale
            ctx = ctx - slope * dist[:, part * tok : (part + 1) * tok]
            scores.append(jnp.where(valid[:, part * tok : (part + 1) * tok], ctx, -1e30))
        near = lax.dot_general(query, fresh_key, nt, preferred_element_type=jnp.float32) * scale
        scores.append(jnp.where(near_ok, near - slope * near_dist, -1e30))
        top = functools.reduce(jnp.maximum, [jnp.max(s, axis=1, keepdims=True) for s in scores])
        exps = [jnp.exp(s - top) for s in scores]
        total = sum(jnp.sum(e, axis=1, keepdims=True) for e in exps)
        weights = [(e / total).astype(jnp.bfloat16) for e in exps]
        values = [ref[:, cols + head * HS : cols + (head + 1) * HS] for ref in (own_ref, far_ref)]
        values.append(fresh_value)
        out = sum(
            jnp.dot(w, v, preferred_element_type=jnp.float32) for w, v in zip(weights, values)
        )
        out = out.astype(out_ref.dtype)
        for r in range(rows // steps):
            out_ref[r, :, head * HS : (head + 1) * HS] = out[r * steps : (r + 1) * steps]


def on_device(hidden, slot_tokens, lengths, decode_rows, query_weight, key_weight, value_weight):
    group = lax.axis_index("head")
    owner = lax.axis_index("pre")
    n = lax.axis_size("head")
    own_tok, width = hidden.shape
    depth = key_weight.shape[0]
    cols = key_weight.shape[1]
    heads_dev = cols // HS
    req_dev, steps = lengths.shape[1], decode_rows.shape[1]
    rows_dev = req_dev * steps
    swap = [(0, 1), (1, 0)]

    order = ring_order(n)
    up = [(order[i], order[(i + 1) % n]) for i in range(n)]
    down = [(order[i], order[(i - 1) % n]) for i in range(n)]
    place = [0] * n
    for i, g in enumerate(order):
        place[g] = i
    half = width // 2
    block = 896 if depth % 896 == 0 else depth

    own = [hidden[:, :half], hidden[:, half:]]
    seen = [((0, 0), (0, 1))] + [
        ((-(k // 2 + 1), k % 2), (k // 2 + 1, 1 - k % 2)) for k in range(n - 1)
    ]
    table = np.zeros((2 * n, 4 * len(seen)), np.int32)
    for g in range(n):
        for k, (distance, part) in enumerate(sum(seen, ())):
            row = order[(place[g] + distance) % n] * width + part * half
            for p in range(2):
                table[2 * g + p, 2 * k : 2 * k + 2] = row % depth, row // depth != p
    rows_of = lax.dynamic_slice_in_dim(jnp.asarray(table), 2 * group + owner, 1, 0)[0]

    def send(pair):
        moving.append((lax.ppermute(pair[0], "head", up), lax.ppermute(pair[1], "head", down)))

    tie = lax.optimization_barrier
    moving = []
    for k in range(2):
        send((own[k % 2], own[1 - k % 2]))
    sums = decode(decode_rows, (query_weight, key_weight, value_weight), block)
    key_far = lax.ppermute(key_weight, "pre", swap)
    moving[0], key_far, second, sums, slot_tokens, lengths = tie(
        (moving[0], key_far, value_weight, sums, slot_tokens, lengths)
    )
    send(moving[0])
    weights = (key_weight, value_weight, key_far, lax.ppermute(second, "pre", swap))

    mine = lax.dynamic_slice_in_dim(slot_tokens, owner * own_tok, own_tok)
    lane = jnp.arange(2 * own_tok, dtype=jnp.int32)
    token = (lane + owner * own_tok) % (2 * own_tok)
    slot = jnp.arange(1, own_tok + 1, dtype=jnp.int32)
    where = jnp.sum(jnp.where(mine[:, None] == token[None, :], slot[:, None], 0), axis=0, keepdims=True)
    lens = lengths[0]
    starts = jnp.cumsum(lens) - lens
    where = jnp.where(where == 0, -(1 << 20), where - 1)
    span = jnp.repeat(jnp.stack([starts, lens], axis=1), steps, axis=0)
    heads_index = (group * heads_dev + jnp.arange(heads_dev)).astype(jnp.float32)
    slope = jnp.exp2(-8.0 * (heads_index + 1.0) / (heads_dev * n))

    moving[1], sums, where, span, slope = tie((moving[1], sums, where, span, slope))
    send(moving[1])
    keep = lax.dynamic_slice_in_dim(sums, owner * rows_dev, rows_dev, 0)
    give = lax.dynamic_slice_in_dim(sums, (1 - owner) * rows_dev, rows_dev, 0)

    moving[2], weights, keep, give = tie((moving[2], weights, keep, give))
    fresh = (keep + lax.ppermute(give, "pre", swap)).astype(jnp.bfloat16)
    (now,) = step([], None, None, rows_of, 0, weights, half)
    acc = jnp.zeros((8, 128), jnp.float32)
    waiting, done = [own] + moving[:2], 0
    for k in range(2, n - 1):
        if k > 2:
            moving[k], acc, now, fresh = tie((moving[k], acc, now, fresh))
        if k + 2 < n - 1:
            send(moving[k])
        waiting.append(moving[k])
        for _ in range(2 if len(waiting) > 1 else 1):
            if len(waiting) > 1 or k < n - 2:
                done += 1
                acc, now = step(waiting.pop(0), acc, now, rows_of, 2 * done, weights, half)
    (acc,) = step(waiting[0], acc, now, rows_of, -1, weights, half, jnp.bfloat16)
    far = lax.ppermute(acc, "pre", swap)
    vmem = pl.BlockSpec(memory_space=pltpu.VMEM)
    return pl.pallas_call(
        functools.partial(attend_kernel, steps),
        out_shape=jax.ShapeDtypeStruct((req_dev, steps, cols), jnp.bfloat16),
        in_specs=[pl.BlockSpec(memory_space=pltpu.SMEM)] + [vmem] * 5,
        out_specs=vmem,
        compiler_params=pltpu.CompilerParams(vmem_limit_bytes=16 * 1024 * 1024),
    )(slope, fresh, acc, far, where, span)


def solution(mesh):
    in_specs = (
        P(("grp", "pre"), "head"),
        P("grp"),
        P(("grp", "pre"), None),
        P("grp", None, "pre"),
        P("pre", "head"),
        P("pre", "head"),
        P("pre", "head"),
    )
    out_specs = P(("grp", "pre"), None, "head")
    return jax.shard_map(
        on_device, mesh=mesh, in_specs=in_specs, out_specs=out_specs, check_vma=False
    )
```

```python
import functools

import jax
import jax.numpy as jnp
import numpy as np
from jax import lax
from jax.experimental import pallas as pl
from jax.experimental.pallas import tpu as pltpu
from jax.sharding import PartitionSpec as P

HS = 128


def ring_order(n):
    if n == 8:
        return [0, 2, 4, 6, 7, 5, 3, 1]
    return list(range(n))


def step_kernel(count, first, rows_ref, *refs):
    more = first >= 0
    items, refs = refs[:count], refs[count:]
    if count:
        acc_ref, now_ref, refs = refs[0], refs[1], refs[2:]
    if more:
        near, far = refs[:2], refs[2:4]
        next_ref, sems = refs[-2:]
        depth = next_ref.shape[1]
        cols = near[0].shape[1]

        def copies(i, sources):
            start = pl.multiple_of(rows_ref[2 * (first + i)], 32)
            return [
                pltpu.make_async_copy(
                    src.at[pl.ds(start, depth), :],
                    next_ref.at[i, :, pl.ds(part * cols, cols)],
                    sems.at[i, part],
                )
                for part, src in enumerate(sources)
            ]

        for i in range(2):

            @pl.when(rows_ref[2 * (first + i) + 1] == 0)
            def _():
                for copy in copies(i, near):
                    copy.start()

            @pl.when(rows_ref[2 * (first + i) + 1] != 0)
            def _():
                for copy in copies(i, far):
                    copy.start()

    if count:
        out_ref = refs[4] if more else refs[0]
        total = acc_ref[...] if acc_ref.shape[0] == items[0].shape[0] else 0.0
        for i in range(count):
            total = total + jnp.dot(items[i][...], now_ref[i], preferred_element_type=jnp.float32)
        out_ref[...] = total.astype(out_ref.dtype)
    if more:
        for i in range(2):
            for copy in copies(i, near):
                copy.wait()


def step(items, acc, now, rows, first, weights, depth, dtype=jnp.float32):
    count, more = len(items), first >= 0
    cols = 2 * weights[0].shape[1]
    vmem = pl.BlockSpec(memory_space=pltpu.VMEM)
    operands, specs = [rows, *items], [pl.BlockSpec(memory_space=pltpu.SMEM)] + [vmem] * count
    shapes = []
    if count:
        tok = items[0].shape[0]
        operands += [acc, now]
        specs += [vmem] * 2
        shapes.append(jax.ShapeDtypeStruct((tok, cols), dtype))
    if more:
        operands += weights
        specs += [pl.BlockSpec(memory_space=pl.ANY)] * 4
        shapes.append(jax.ShapeDtypeStruct((2, depth, cols), jnp.bfloat16))
    return pl.pallas_call(
        functools.partial(step_kernel, count, first),
        out_shape=shapes,
        in_specs=specs,
        out_specs=[vmem] * len(shapes),
        scratch_shapes=[pltpu.SemaphoreType.DMA((2, 2))] if more else [],
        compiler_params=pltpu.CompilerParams(vmem_limit_bytes=40 * 1024 * 1024),
        cost_estimate=pl.CostEstimate(flops=0, bytes_accessed=0, transcendentals=0),
    )(*operands)


def decode_kernel(rows_ref, wq_ref, wk_ref, wv_ref, out_ref, flat):
    count, steps, _ = rows_ref.shape
    cols = wq_ref.shape[1]
    for r in range(count):
        flat[r * steps : (r + 1) * steps] = rows_ref[r].astype(jnp.float32)
    rows = flat[...].astype(jnp.bfloat16)
    for part, ref in enumerate((wq_ref, wk_ref, wv_ref)):
        term = jnp.dot(rows, ref[...], preferred_element_type=jnp.float32)
        at = slice(part * cols, (part + 1) * cols)

        @pl.when(pl.program_id(0) == 0)
        def _():
            out_ref[:, at] = term

        @pl.when(pl.program_id(0) != 0)
        def _():
            out_ref[:, at] += term


def decode(rows, weights, block):
    count, steps, depth = rows.shape
    cols = weights[0].shape[1]
    return pl.pallas_call(
        decode_kernel,
        out_shape=jax.ShapeDtypeStruct((count * steps, 3 * cols), jnp.float32),
        grid=(depth // block,),
        in_specs=[pl.BlockSpec((count, steps, block), lambda i: (0, 0, i))]
        + [pl.BlockSpec((block, cols), lambda i: (i, 0))] * 3,
        out_specs=pl.BlockSpec((count * steps, 3 * cols), lambda i: (0, 0)),
        scratch_shapes=[pltpu.VMEM((count * steps, block), jnp.float32)],
        compiler_params=pltpu.CompilerParams(vmem_limit_bytes=56 * 1024 * 1024),
        cost_estimate=pl.CostEstimate(flops=0, bytes_accessed=0, transcendentals=0),
    )(rows, *weights)


def plan_kernel(steps, owner_ref, slope_ref, sums_ref, far_ref, place_ref, span_ref, fresh_ref, bias_ref):
    rows, cols = fresh_ref.shape
    mine = pl.ds(pl.multiple_of(owner_ref[0] * rows, 8), rows)
    fresh_ref[...] = (sums_ref[mine, :] + far_ref[mine, :]).astype(fresh_ref.dtype)
    start = span_ref[:, 0:1]
    length = span_ref[:, 1:2]
    row = lax.broadcasted_iota(jnp.int32, (rows, 1), 0)
    rel = place_ref[...] - start
    valid = (rel >= 0) & (rel < length)
    dist = (length + row % steps - rel).astype(jnp.float32)
    col = lax.broadcasted_iota(jnp.int32, (1, rows), 1)
    near_ok = (row // steps == col // steps) & (col <= row)
    near_dist = (row - col).astype(jnp.float32)
    slots = place_ref.shape[1]
    for head in range(bias_ref.shape[0]):
        bias_ref[head, :, :slots] = jnp.where(valid, -(slope_ref[head] * dist), -1e30)
        bias_ref[head, :, slots:] = jnp.where(near_ok, -(slope_ref[head] * near_dist), -1e30)


def attend_kernel(steps, fresh_ref, own_ref, far_ref, bias_ref, out_ref):
    rows = fresh_ref.shape[0]
    cols = fresh_ref.shape[1] // 3
    scale = 1.0 / HS**0.5
    nt = (((1,), (1,)), ((), ()))
    heads = range(cols // HS)
    fresh = fresh_ref[:, cols:]
    scores, out = [], []
    for head in heads:
        query = fresh_ref[:, head * HS : (head + 1) * HS]
        at, here = 0, []
        for part in (own_ref, far_ref, fresh):
            key = part[:, head * HS : (head + 1) * HS]
            score = lax.dot_general(query, key, nt, preferred_element_type=jnp.float32) * scale
            here.append(score + bias_ref[head, :, at : at + score.shape[1]])
            at += score.shape[1]
        scores.append(here)
    for head in heads:
        top = functools.reduce(jnp.maximum, [jnp.max(s, axis=1, keepdims=True) for s in scores[head]])
        exps = [jnp.exp(s - top) for s in scores[head]]
        total = 1.0 / sum(jnp.sum(e, axis=1, keepdims=True) for e in exps)
        weights = [(e * total).astype(jnp.bfloat16) for e in exps]
        values = [part[:, cols + head * HS : cols + (head + 1) * HS] for part in (own_ref, far_ref, fresh)]
        out.append(sum(jnp.dot(w, v, preferred_element_type=jnp.float32) for w, v in zip(weights, values)))
    for head in heads:
        for r in range(rows // steps):
            out_ref[r, :, head * HS : (head + 1) * HS] = out[head][r * steps : (r + 1) * steps].astype(out_ref.dtype)


def on_device(hidden, slot_tokens, lengths, decode_rows, query_weight, key_weight, value_weight):
    group = lax.axis_index("head")
    owner = lax.axis_index("pre")
    n = lax.axis_size("head")
    own_tok, width = hidden.shape
    depth = key_weight.shape[0]
    cols = key_weight.shape[1]
    heads_dev = cols // HS
    req_dev, steps = lengths.shape[1], decode_rows.shape[1]
    rows_dev = req_dev * steps
    swap = [(0, 1), (1, 0)]

    order = ring_order(n)
    up = [(order[i], order[(i + 1) % n]) for i in range(n)]
    down = [(order[i], order[(i - 1) % n]) for i in range(n)]
    place = [0] * n
    for i, g in enumerate(order):
        place[g] = i
    half = width // 2
    block = depth // 2

    own = [hidden[:, :half], hidden[:, half:]]
    seen = [((0, 0), (0, 1))] + [
        ((-(k // 2 + 1), k % 2), (k // 2 + 1, 1 - k % 2)) for k in range(n - 1)
    ]
    table = np.zeros((2 * n, 4 * len(seen)), np.int32)
    for g in range(n):
        for k, (distance, part) in enumerate(sum(seen, ())):
            row = order[(place[g] + distance) % n] * width + part * half
            for p in range(2):
                table[2 * g + p, 2 * k : 2 * k + 2] = row % depth, row // depth != p
    rows_of = lax.dynamic_slice_in_dim(jnp.asarray(table), 2 * group + owner, 1, 0)[0]

    def send(pair):
        moving.append((lax.ppermute(pair[0], "head", up), lax.ppermute(pair[1], "head", down)))

    tie = lax.optimization_barrier
    moving = []
    for k in range(2):
        send((own[k % 2], own[1 - k % 2]))
    sums = decode(decode_rows, (query_weight, key_weight, value_weight), block)
    weights = (key_weight, value_weight) + tuple(lax.ppermute(w, "pre", swap) for w in (key_weight, value_weight))
    moving[0], sums, slot_tokens, lengths = tie((moving[0], sums, slot_tokens, lengths))
    send(moving[0])

    mine = lax.dynamic_slice_in_dim(slot_tokens, owner * own_tok, own_tok)
    lane = jnp.arange(2 * own_tok, dtype=jnp.int32)
    token = (lane + owner * own_tok) % (2 * own_tok)
    slot = jnp.arange(1, own_tok + 1, dtype=jnp.int32)
    where = jnp.sum(jnp.where(mine[:, None] == token[None, :], slot[:, None], 0), axis=0, keepdims=True)
    lens = lengths[0]
    starts = jnp.cumsum(lens) - lens
    where = jnp.where(where == 0, -(1 << 20), where - 1)
    span = jnp.repeat(jnp.stack([starts, lens], axis=1), steps, axis=0)
    heads_index = (group * heads_dev + jnp.arange(heads_dev)).astype(jnp.float32)
    slope = jnp.exp2(-8.0 * (heads_index + 1.0) / (heads_dev * n))

    moving[1], weights, sums, where, span, slope = tie((moving[1], weights, sums, where, span, slope))
    send(moving[1])
    sums_far = lax.ppermute(sums, "pre", swap)
    (now,) = step([], None, None, rows_of, 0, weights, half)
    acc = jnp.zeros((8, 128), jnp.float32)
    waiting, done = [own, moving[0]], 0
    vmem = pl.BlockSpec(memory_space=pltpu.VMEM)
    smem = pl.BlockSpec(memory_space=pltpu.SMEM)
    for k in range(1, n - 2):
        if k == 2:
            moving[k], acc, now, sums_far = tie((moving[k], acc, now, sums_far))
        elif k > 2:
            moving[k], acc, now = tie((moving[k], acc, now))
        if 1 < k < n - 3:
            send(moving[k])
        waiting.append(moving[k])
        for _ in range(min(len(waiting), 1 if k == 1 else 2)):
            done += 1
            acc, now = step(waiting.pop(0), acc, now, rows_of, 2 * done, weights, half)
        if k == 4:
            fresh, bias = pl.pallas_call(
                functools.partial(plan_kernel, steps),
                out_shape=[
                    jax.ShapeDtypeStruct((rows_dev, 3 * cols), jnp.bfloat16),
                    jax.ShapeDtypeStruct((heads_dev, rows_dev, 2 * own_tok + rows_dev), jnp.float32),
                ],
                in_specs=[smem] * 2 + [vmem] * 4,
                out_specs=[vmem] * 2,
                compiler_params=pltpu.CompilerParams(vmem_limit_bytes=16 * 1024 * 1024),
                cost_estimate=pl.CostEstimate(flops=0, bytes_accessed=0, transcendentals=0),
            )(owner[None], slope, sums, sums_far, where, span)
            acc, fresh, bias = tie((acc, fresh, bias))
    (acc,) = step(moving[n - 2], acc, now, rows_of, -1, weights, half, jnp.bfloat16)
    far = lax.ppermute(acc, "pre", swap)
    return pl.pallas_call(
        functools.partial(attend_kernel, steps),
        out_shape=jax.ShapeDtypeStruct((req_dev, steps, cols), jnp.bfloat16),
        in_specs=[vmem] * 4,
        out_specs=vmem,
        compiler_params=pltpu.CompilerParams(vmem_limit_bytes=16 * 1024 * 1024),
    )(fresh, acc, far, bias)


def solution(mesh):
    in_specs = (
        P(("grp", "pre"), "head"),
        P("grp"),
        P(("grp", "pre"), None),
        P("grp", None, "pre"),
        P("pre", "head"),
        P("pre", "head"),
        P("pre", "head"),
    )
    out_specs = P(("grp", "pre"), None, "head")
    return jax.shard_map(
        on_device, mesh=mesh, in_specs=in_specs, out_specs=out_specs, check_vma=False
    )
```

```python
import functools

import jax
import jax.numpy as jnp
import numpy as np
from jax import lax
from jax.experimental import pallas as pl
from jax.experimental.pallas import tpu as pltpu
from jax.sharding import PartitionSpec as P

HS = 128


def ring_order(n):
    if n == 8:
        return [0, 2, 4, 6, 7, 5, 3, 1]
    return list(range(n))


def step_kernel(parts, block, rows_ref, *refs):
    items, refs = refs[: len(parts)], refs[len(parts) :]
    if parts:
        acc_ref, now_ref, refs = refs[0], refs[1], refs[2:]
    if block is not None:
        near, far = refs[:2], refs[2:4]
        next_ref, sems = refs[-2:]
        depth = next_ref.shape[0]
        cols = near[0].shape[1]

        def copies(sources):
            start = pl.multiple_of(rows_ref[2 * block], 64)
            return [
                pltpu.make_async_copy(
                    src.at[pl.ds(start, depth), :], next_ref.at[:, pl.ds(part * cols, cols)], sems.at[part]
                )
                for part, src in enumerate(sources)
            ]

        @pl.when(rows_ref[2 * block + 1] == 0)
        def _():
            for copy in copies(near):
                copy.start()

        @pl.when(rows_ref[2 * block + 1] != 0)
        def _():
            for copy in copies(far):
                copy.start()

    if parts:
        out_ref = refs[0] if block is None else refs[4]
        total = acc_ref[...] if acc_ref.shape == out_ref.shape else 0.0
        for item, at in zip(items, parts):
            rows = now_ref[at : at + item.shape[1], :]
            total = total + jnp.dot(item[...], rows, preferred_element_type=jnp.float32)
        out_ref[...] = total.astype(out_ref.dtype)
    if block is not None:
        for copy in copies(near):
            copy.wait()


def step(items, parts, acc, now, rows, block, weights, depth, dtype=jnp.float32, flops=0):
    cols = 2 * weights[0].shape[1]
    vmem = pl.BlockSpec(memory_space=pltpu.VMEM)
    operands, specs = [rows, *items], [pl.BlockSpec(memory_space=pltpu.SMEM)] + [vmem] * len(items)
    shapes, scratch = [], []
    if items:
        operands += [acc, now]
        specs += [vmem] * 2
        shapes.append(jax.ShapeDtypeStruct((items[0].shape[0], cols), dtype))
    if block is not None:
        operands += weights
        specs += [pl.BlockSpec(memory_space=pl.ANY)] * 4
        shapes.append(jax.ShapeDtypeStruct((depth, cols), jnp.bfloat16))
        scratch.append(pltpu.SemaphoreType.DMA((2,)))
    return pl.pallas_call(
        functools.partial(step_kernel, parts, block),
        out_shape=shapes,
        in_specs=specs,
        out_specs=[vmem] * len(shapes),
        scratch_shapes=scratch,
        compiler_params=pltpu.CompilerParams(vmem_limit_bytes=46 * 1024 * 1024),
        cost_estimate=pl.CostEstimate(flops=flops, bytes_accessed=0, transcendentals=0),
    )(*operands)


def decode_kernel(rows_ref, weight_ref, out_ref, flat):
    count, steps, _ = rows_ref.shape
    for r in range(count):
        flat[r * steps : (r + 1) * steps] = rows_ref[r].astype(jnp.float32)
    rows = flat[...].astype(jnp.bfloat16)
    term = jnp.dot(rows, weight_ref[...], preferred_element_type=jnp.float32)

    @pl.when(pl.program_id(0) == 0)
    def _():
        out_ref[...] = term

    @pl.when(pl.program_id(0) != 0)
    def _():
        out_ref[...] += term


def decode(rows, weight, block):
    count, steps, depth = rows.shape
    cols = weight.shape[1]
    return pl.pallas_call(
        decode_kernel,
        out_shape=jax.ShapeDtypeStruct((count * steps, cols), jnp.float32),
        grid=(depth // block,),
        in_specs=[
            pl.BlockSpec((count, steps, block), lambda i: (0, 0, i)),
            pl.BlockSpec((block, cols), lambda i: (i, 0)),
        ],
        out_specs=pl.BlockSpec((count * steps, cols), lambda i: (0, 0)),
        scratch_shapes=[pltpu.VMEM((count * steps, block), jnp.float32)],
        compiler_params=pltpu.CompilerParams(vmem_limit_bytes=52 * 1024 * 1024),
        cost_estimate=pl.CostEstimate(flops=0, bytes_accessed=0, transcendentals=0),
    )(rows, weight)


def plan_kernel(steps, owner_ref, slope_ref, place_ref, span_ref, *refs):
    sums, (fresh_ref, bias_ref) = refs[:-2], refs[-2:]
    rows = fresh_ref.shape[0]
    cols = sums[0].shape[1]
    mine = pl.ds(pl.multiple_of(owner_ref[0] * rows, 8), rows)
    for part in range(3):
        both = sums[part][mine, :] + sums[part + 3][mine, :]
        fresh_ref[:, part * cols : (part + 1) * cols] = both.astype(fresh_ref.dtype)
    start = span_ref[:, 0:1]
    length = span_ref[:, 1:2]
    row = lax.broadcasted_iota(jnp.int32, (rows, 1), 0)
    rel = place_ref[...] - start
    valid = (rel >= 0) & (rel < length)
    dist = (length + row % steps - rel).astype(jnp.float32)
    col = lax.broadcasted_iota(jnp.int32, (1, rows), 1)
    near_ok = (row // steps == col // steps) & (col <= row)
    near_dist = (row - col).astype(jnp.float32)
    slots = place_ref.shape[1]
    for head in range(bias_ref.shape[0]):
        bias_ref[head, :, :slots] = jnp.where(valid, -(slope_ref[head] * dist), -1e30)
        bias_ref[head, :, slots:] = jnp.where(near_ok, -(slope_ref[head] * near_dist), -1e30)


def attend_kernel(steps, fresh_ref, own_ref, far_ref, bias_ref, out_ref):
    rows = fresh_ref.shape[0]
    cols = fresh_ref.shape[1] // 3
    scale = 1.0 / HS**0.5
    nt = (((1,), (1,)), ((), ()))
    heads = range(cols // HS)
    fresh = fresh_ref[:, cols:]
    scores, out = [], []
    for head in heads:
        query = fresh_ref[:, head * HS : (head + 1) * HS]
        at, here = 0, []
        for part in (own_ref, far_ref, fresh):
            key = part[:, head * HS : (head + 1) * HS]
            score = lax.dot_general(query, key, nt, preferred_element_type=jnp.float32) * scale
            here.append(score + bias_ref[head, :, at : at + score.shape[1]])
            at += score.shape[1]
        scores.append(here)
    for head in heads:
        top = functools.reduce(jnp.maximum, [jnp.max(s, axis=1, keepdims=True) for s in scores[head]])
        exps = [jnp.exp(s - top) for s in scores[head]]
        total = 1.0 / sum(jnp.sum(e, axis=1, keepdims=True) for e in exps)
        weights = [(e * total).astype(jnp.bfloat16) for e in exps]
        values = [part[:, cols + head * HS : cols + (head + 1) * HS] for part in (own_ref, far_ref, fresh)]
        out.append(sum(jnp.dot(w, v, preferred_element_type=jnp.float32) for w, v in zip(weights, values)))
    for head in heads:
        for r in range(rows // steps):
            out_ref[r, :, head * HS : (head + 1) * HS] = out[head][r * steps : (r + 1) * steps].astype(out_ref.dtype)


def on_device(hidden, slot_tokens, lengths, decode_rows, query_weight, key_weight, value_weight):
    group = lax.axis_index("head")
    owner = lax.axis_index("pre")
    n = lax.axis_size("head")
    own_tok, width = hidden.shape
    depth = key_weight.shape[0]
    cols = key_weight.shape[1]
    heads_dev = cols // HS
    req_dev, steps = lengths.shape[1], decode_rows.shape[1]
    rows_dev = req_dev * steps
    swap = [(0, 1), (1, 0)]

    order = ring_order(n)
    around = [(order[i], order[(i + 1) % n]) for i in range(n)]
    around += [(n + order[i], n + order[(i - 1) % n]) for i in range(n)]
    table = np.zeros((2 * n, 2 * n), np.int32)
    for g in range(n):
        for p in range(2):
            for hop in range(n):
                row = order[(order.index(g) + (hop if p else -hop)) % n] * width
                table[2 * g + p, 2 * hop : 2 * hop + 2] = row % depth, row // depth != p
    rows_of = lax.dynamic_slice_in_dim(jnp.asarray(table), 2 * group + owner, 1, 0)[0]

    tie = lax.optimization_barrier
    cut = width // 2
    parts = (0, cut)
    own = [hidden[:, :cut], hidden[:, cut:]]

    def send(item):
        return lax.ppermute(item, ("pre", "head"), around)

    moving = [send(own[0]), send(own[1])]
    weights = (key_weight, value_weight) + tuple(lax.ppermute(w, "pre", swap) for w in (key_weight, value_weight))
    sums = [decode(decode_rows, query_weight, depth // 2)]
    moving[0], sums[0], decode_rows, slot_tokens, lengths = tie(
        (moving[0], sums[0], decode_rows, slot_tokens, lengths)
    )
    moving.append(send(moving[0]))
    mine = lax.dynamic_slice_in_dim(slot_tokens, owner * own_tok, own_tok)
    lane = jnp.arange(2 * own_tok, dtype=jnp.int32)
    token = (lane + owner * own_tok) % (2 * own_tok)
    slot = jnp.arange(1, own_tok + 1, dtype=jnp.int32)
    where = jnp.sum(jnp.where(mine[:, None] == token[None, :], slot[:, None], 0), axis=0, keepdims=True)
    lens = lengths[0]
    starts = jnp.cumsum(lens) - lens
    where = jnp.where(where == 0, -(1 << 20), where - 1)
    span = jnp.repeat(jnp.stack([starts, lens], axis=1), steps, axis=0)
    heads_index = (group * heads_dev + jnp.arange(heads_dev)).astype(jnp.float32)
    slope = jnp.exp2(-8.0 * (heads_index + 1.0) / (heads_dev * n))

    moving[1], where, span, slope, rows_of = tie((moving[1], where, span, slope, rows_of))
    moving.append(send(moving[1]))
    sums.append(decode(decode_rows, key_weight, depth // 2))
    moving[2], weights, sums[1] = tie((moving[2], weights, sums[1]))
    moving.append(send(moving[2]))
    (now,) = step([], (), None, None, rows_of, 0, weights, width)
    acc = jnp.zeros((8, 128), jnp.float32)
    vmem = pl.BlockSpec(memory_space=pltpu.VMEM)
    smem = pl.BlockSpec(memory_space=pltpu.SMEM)
    done = 0
    for k in range(3, 2 * n - 2):
        moving[k], acc, now = tie((moving[k], acc, now))
        if k + 2 < 2 * n - 2:
            moving.append(send(moving[k]))
        if k == 3:
            decode_rows, acc = tie((decode_rows, acc))
            sums.append(decode(decode_rows, value_weight, depth // 2))
            acc, now, sums[2] = tie((acc, now, sums[2]))
            sums_far = [lax.ppermute(part, "pre", swap) for part in sums]
            continue
        if done < n - 1 and 2 * done <= k + 1 and k not in (9,):
            items = moving[2 * done - 2 : 2 * done] if done else own
            done += 1
            acc, now = step(items, parts, acc, now, rows_of, done, weights, width)
        if k == 9:
            fresh, bias = pl.pallas_call(
                functools.partial(plan_kernel, steps),
                out_shape=[
                    jax.ShapeDtypeStruct((rows_dev, 3 * cols), jnp.bfloat16),
                    jax.ShapeDtypeStruct((heads_dev, rows_dev, 2 * own_tok + rows_dev), jnp.float32),
                ],
                in_specs=[smem] * 2 + [vmem] * 8,
                out_specs=[vmem] * 2,
                compiler_params=pltpu.CompilerParams(vmem_limit_bytes=8 * 1024 * 1024),
                cost_estimate=pl.CostEstimate(flops=0, bytes_accessed=0, transcendentals=0),
            )(owner[None], slope, where, span, *sums, *sums_far)
            acc, fresh, bias = tie((acc, fresh, bias))
    (acc,) = step(moving[-2:], parts, acc, now, rows_of, None, weights, width, jnp.bfloat16)
    far = lax.ppermute(acc, "pre", swap)
    return pl.pallas_call(
        functools.partial(attend_kernel, steps),
        out_shape=jax.ShapeDtypeStruct((req_dev, steps, cols), jnp.bfloat16),
        in_specs=[vmem] * 4,
        out_specs=vmem,
        compiler_params=pltpu.CompilerParams(vmem_limit_bytes=16 * 1024 * 1024),
    )(fresh, acc, far, bias)


def solution(mesh):
    in_specs = (
        P(("grp", "pre"), "head"),
        P("grp"),
        P(("grp", "pre"), None),
        P("grp", None, "pre"),
        P("pre", "head"),
        P("pre", "head"),
        P("pre", "head"),
    )
    out_specs = P(("grp", "pre"), None, "head")
    return jax.shard_map(
        on_device, mesh=mesh, in_specs=in_specs, out_specs=out_specs, check_vma=False
    )
```

```python
import functools

import jax
import jax.numpy as jnp
import numpy as np
from jax import lax
from jax.experimental import pallas as pl
from jax.experimental.pallas import tpu as pltpu
from jax.sharding import PartitionSpec as P

HS = 128


def ring_order(n):
    if n == 8:
        return [0, 2, 4, 6, 7, 5, 3, 1]
    return list(range(n))


def step_kernel(parts, block, rows_ref, *refs):
    items, refs = refs[: len(parts)], refs[len(parts) :]
    if parts:
        acc_ref, now_ref, refs = refs[0], refs[1], refs[2:]
    if block is not None:
        near, far = refs[:2], refs[2:4]
        next_ref, sems = refs[-2:]
        depth = next_ref.shape[0]
        cols = near[0].shape[1]

        def copies(sources):
            start = pl.multiple_of(rows_ref[2 * block], 64)
            return [
                pltpu.make_async_copy(
                    src.at[pl.ds(start, depth), :], next_ref.at[:, pl.ds(part * cols, cols)], sems.at[part]
                )
                for part, src in enumerate(sources)
            ]

        @pl.when(rows_ref[2 * block + 1] == 0)
        def _():
            for copy in copies(near):
                copy.start()

        @pl.when(rows_ref[2 * block + 1] != 0)
        def _():
            for copy in copies(far):
                copy.start()

    if parts:
        out_ref = refs[0] if block is None else refs[4]
        total = acc_ref[...] if acc_ref.shape == out_ref.shape else 0.0
        for item, at in zip(items, parts):
            rows = now_ref[at : at + item.shape[1], :]
            total = total + jnp.dot(item[...], rows, preferred_element_type=jnp.float32)
        out_ref[...] = total.astype(out_ref.dtype)
    if block is not None:
        for copy in copies(near):
            copy.wait()


def step(items, parts, acc, now, rows, block, weights, depth, dtype=jnp.float32, flops=0):
    cols = 2 * weights[0].shape[1]
    vmem = pl.BlockSpec(memory_space=pltpu.VMEM)
    operands, specs = [rows, *items], [pl.BlockSpec(memory_space=pltpu.SMEM)] + [vmem] * len(items)
    shapes, scratch = [], []
    if items:
        operands += [acc, now]
        specs += [vmem] * 2
        shapes.append(jax.ShapeDtypeStruct((items[0].shape[0], cols), dtype))
    if block is not None:
        operands += weights
        specs += [pl.BlockSpec(memory_space=pl.ANY)] * 4
        shapes.append(jax.ShapeDtypeStruct((depth, cols), jnp.bfloat16))
        scratch.append(pltpu.SemaphoreType.DMA((2,)))
    return pl.pallas_call(
        functools.partial(step_kernel, parts, block),
        out_shape=shapes,
        in_specs=specs,
        out_specs=[vmem] * len(shapes),
        scratch_shapes=scratch,
        compiler_params=pltpu.CompilerParams(vmem_limit_bytes=46 * 1024 * 1024),
        cost_estimate=pl.CostEstimate(flops=flops, bytes_accessed=0, transcendentals=0),
    )(*operands)


def decode_kernel(rows_ref, weight_ref, out_ref, flat):
    count, steps, _ = rows_ref.shape
    for r in range(count):
        flat[r * steps : (r + 1) * steps] = rows_ref[r].astype(jnp.float32)
    rows = flat[...].astype(jnp.bfloat16)
    term = jnp.dot(rows, weight_ref[...], preferred_element_type=jnp.float32)

    @pl.when(pl.program_id(0) == 0)
    def _():
        out_ref[...] = term

    @pl.when(pl.program_id(0) != 0)
    def _():
        out_ref[...] += term


def decode(rows, weight, block):
    count, steps, depth = rows.shape
    cols = weight.shape[1]
    return pl.pallas_call(
        decode_kernel,
        out_shape=jax.ShapeDtypeStruct((count * steps, cols), jnp.float32),
        grid=(depth // block,),
        in_specs=[
            pl.BlockSpec((count, steps, block), lambda i: (0, 0, i)),
            pl.BlockSpec((block, cols), lambda i: (i, 0)),
        ],
        out_specs=pl.BlockSpec((count * steps, cols), lambda i: (0, 0)),
        scratch_shapes=[pltpu.VMEM((count * steps, block), jnp.float32)],
        compiler_params=pltpu.CompilerParams(vmem_limit_bytes=52 * 1024 * 1024),
        cost_estimate=pl.CostEstimate(flops=0, bytes_accessed=0, transcendentals=0),
    )(rows, weight)


def plan_kernel(steps, owner_ref, slope_ref, place_ref, span_ref, *refs):
    sums, (fresh_ref, bias_ref) = refs[:-2], refs[-2:]
    rows = fresh_ref.shape[0]
    cols = sums[0].shape[1]
    mine = pl.ds(pl.multiple_of(owner_ref[0] * rows, 8), rows)
    for part in range(3):
        both = sums[part][mine, :] + sums[part + 3][mine, :]
        fresh_ref[:, part * cols : (part + 1) * cols] = both.astype(fresh_ref.dtype)
    start = span_ref[:, 0:1]
    length = span_ref[:, 1:2]
    row = lax.broadcasted_iota(jnp.int32, (rows, 1), 0)
    rel = place_ref[...] - start
    valid = (rel >= 0) & (rel < length)
    dist = (length + row % steps - rel).astype(jnp.float32)
    col = lax.broadcasted_iota(jnp.int32, (1, rows), 1)
    near_ok = (row // steps == col // steps) & (col <= row)
    near_dist = (row - col).astype(jnp.float32)
    slots = place_ref.shape[1]
    for head in range(bias_ref.shape[0]):
        bias_ref[head, :, :slots] = jnp.where(valid, -(slope_ref[head] * dist), -1e30)
        bias_ref[head, :, slots:] = jnp.where(near_ok, -(slope_ref[head] * near_dist), -1e30)


def last_kernel(parts, at, *refs):
    items, (acc_ref, now_ref, out_ref) = refs[: len(parts)], refs[len(parts) :]
    cols = slice(at, at + out_ref.shape[1])
    total = acc_ref[:, cols]
    for item, start in zip(items, parts):
        rows = now_ref[start : start + item.shape[1], cols]
        total = total + jnp.dot(item[...], rows, preferred_element_type=jnp.float32)
    out_ref[...] = total.astype(out_ref.dtype)


def weight_kernel(fresh_ref, own_ref, far_ref, bias_ref, out_ref):
    cols = own_ref.shape[1]
    nt = (((1,), (1,)), ((), ()))
    for head in range(cols // HS):
        at = slice(head * HS, (head + 1) * HS)
        key = fresh_ref[:, cols + head * HS : cols + (head + 1) * HS]
        scores, start = [], 0
        for part in (own_ref[:, at], far_ref[:, at], key):
            score = lax.dot_general(fresh_ref[:, at], part, nt, preferred_element_type=jnp.float32)
            stop = start + score.shape[1]
            scores.append(score * (1.0 / HS**0.5) + bias_ref[head, :, start:stop])
            start = stop
        top = functools.reduce(jnp.maximum, [jnp.max(s, axis=1, keepdims=True) for s in scores])
        exps = [jnp.exp(s - top) for s in scores]
        total = 1.0 / sum(jnp.sum(e, axis=1, keepdims=True) for e in exps)
        start = 0
        for e in exps:
            out_ref[head, :, start : start + e.shape[1]] = (e * total).astype(out_ref.dtype)
            start += e.shape[1]


def value_kernel(steps, weight_ref, fresh_ref, own_ref, far_ref, out_ref):
    rows = fresh_ref.shape[0]
    tok, cols = own_ref.shape
    for head in range(cols // HS):
        at = slice(head * HS, (head + 1) * HS)
        fresh = fresh_ref[:, 2 * cols + head * HS : 2 * cols + (head + 1) * HS]
        out = jnp.dot(weight_ref[head, :, :tok], own_ref[:, at], preferred_element_type=jnp.float32)
        out += jnp.dot(weight_ref[head, :, tok : 2 * tok], far_ref[:, at], preferred_element_type=jnp.float32)
        out += jnp.dot(weight_ref[head, :, 2 * tok :], fresh, preferred_element_type=jnp.float32)
        out_ref[:, :, at] = out.reshape(rows // steps, steps, HS).astype(out_ref.dtype)


def on_device(hidden, slot_tokens, lengths, decode_rows, query_weight, key_weight, value_weight):
    group = lax.axis_index("head")
    owner = lax.axis_index("pre")
    n = lax.axis_size("head")
    own_tok, width = hidden.shape
    depth = key_weight.shape[0]
    cols = key_weight.shape[1]
    heads_dev = cols // HS
    req_dev, steps = lengths.shape[1], decode_rows.shape[1]
    rows_dev = req_dev * steps
    swap = [(0, 1), (1, 0)]

    order = ring_order(n)
    around = [(order[i], order[(i + 1) % n]) for i in range(n)]
    around += [(n + order[i], n + order[(i - 1) % n]) for i in range(n)]
    table = np.zeros((2 * n, 2 * n), np.int32)
    for g in range(n):
        for p in range(2):
            for hop in range(n):
                row = order[(order.index(g) + (hop if p else -hop)) % n] * width
                table[2 * g + p, 2 * hop : 2 * hop + 2] = row % depth, row // depth != p
    rows_of = lax.dynamic_slice_in_dim(jnp.asarray(table), 2 * group + owner, 1, 0)[0]

    tie = lax.optimization_barrier
    cut = width // 2
    parts = (0, cut)
    own = [hidden[:, :cut], hidden[:, cut:]]

    def send(item):
        return lax.ppermute(item, ("pre", "head"), around)

    moving = [send(own[0]), send(own[1])]
    weights = (key_weight, value_weight) + tuple(lax.ppermute(w, "pre", swap) for w in (key_weight, value_weight))
    sums = [decode(decode_rows, query_weight, depth // 2)]
    moving[0], sums[0], decode_rows, slot_tokens, lengths = tie(
        (moving[0], sums[0], decode_rows, slot_tokens, lengths)
    )
    moving.append(send(moving[0]))
    mine = lax.dynamic_slice_in_dim(slot_tokens, owner * own_tok, own_tok)
    lane = jnp.arange(2 * own_tok, dtype=jnp.int32)
    token = (lane + owner * own_tok) % (2 * own_tok)
    slot = jnp.arange(1, own_tok + 1, dtype=jnp.int32)
    where = jnp.sum(jnp.where(mine[:, None] == token[None, :], slot[:, None], 0), axis=0, keepdims=True)
    lens = lengths[0]
    starts = jnp.cumsum(lens) - lens
    where = jnp.where(where == 0, -(1 << 20), where - 1)
    span = jnp.repeat(jnp.stack([starts, lens], axis=1), steps, axis=0)
    heads_index = (group * heads_dev + jnp.arange(heads_dev)).astype(jnp.float32)
    slope = jnp.exp2(-8.0 * (heads_index + 1.0) / (heads_dev * n))

    moving[1], where, span, slope, rows_of = tie((moving[1], where, span, slope, rows_of))
    moving.append(send(moving[1]))
    sums.append(decode(decode_rows, key_weight, depth // 2))
    moving[2], weights, sums[1] = tie((moving[2], weights, sums[1]))
    moving.append(send(moving[2]))
    (now,) = step([], (), None, None, rows_of, 0, weights, width)
    acc = jnp.zeros((8, 128), jnp.float32)
    vmem = pl.BlockSpec(memory_space=pltpu.VMEM)
    smem = pl.BlockSpec(memory_space=pltpu.SMEM)
    done = 0
    for k in range(3, 2 * n - 2):
        moving[k], acc, now = tie((moving[k], acc, now))
        if k + 2 < 2 * n - 2:
            moving.append(send(moving[k]))
        if k == 3:
            decode_rows, acc = tie((decode_rows, acc))
            sums.append(decode(decode_rows, value_weight, depth // 2))
            acc, now, sums[2] = tie((acc, now, sums[2]))
            sums_far = [lax.ppermute(part, "pre", swap) for part in sums]
            continue
        if done < n - 1 and 2 * done <= k + 1 and k not in (9,):
            items = moving[2 * done - 2 : 2 * done] if done else own
            done += 1
            acc, now = step(items, parts, acc, now, rows_of, done, weights, width)
        if k == 9:
            fresh, bias = pl.pallas_call(
                functools.partial(plan_kernel, steps),
                out_shape=[
                    jax.ShapeDtypeStruct((rows_dev, 3 * cols), jnp.bfloat16),
                    jax.ShapeDtypeStruct((heads_dev, rows_dev, 2 * own_tok + rows_dev), jnp.float32),
                ],
                in_specs=[smem] * 2 + [vmem] * 8,
                out_specs=[vmem] * 2,
                compiler_params=pltpu.CompilerParams(vmem_limit_bytes=8 * 1024 * 1024),
                cost_estimate=pl.CostEstimate(flops=0, bytes_accessed=0, transcendentals=0),
            )(owner[None], slope, where, span, *sums, *sums_far)
            acc, fresh, bias = tie((acc, fresh, bias))
    limit = pltpu.CompilerParams(vmem_limit_bytes=16 * 1024 * 1024)
    cost = pl.CostEstimate(flops=0, bytes_accessed=0, transcendentals=0)
    near = [
        pl.pallas_call(
            functools.partial(last_kernel, parts, at),
            out_shape=jax.ShapeDtypeStruct((own_tok, cols), jnp.bfloat16),
            in_specs=[vmem] * 4,
            out_specs=vmem,
            compiler_params=limit,
            cost_estimate=cost,
        )(*moving[-2:], acc, now)
        for at in (0, cols)
    ]
    far = [lax.ppermute(part, "pre", swap) for part in near]
    soft = pl.pallas_call(
        weight_kernel,
        out_shape=jax.ShapeDtypeStruct((heads_dev, rows_dev, 2 * own_tok + rows_dev), jnp.bfloat16),
        in_specs=[vmem] * 4,
        out_specs=vmem,
        compiler_params=limit,
        cost_estimate=cost,
    )(fresh, near[0], far[0], bias)
    return pl.pallas_call(
        functools.partial(value_kernel, steps),
        out_shape=jax.ShapeDtypeStruct((req_dev, steps, cols), jnp.bfloat16),
        in_specs=[vmem] * 4,
        out_specs=vmem,
        compiler_params=limit,
    )(soft, fresh, near[1], far[1])


def solution(mesh):
    in_specs = (
        P(("grp", "pre"), "head"),
        P("grp"),
        P(("grp", "pre"), None),
        P("grp", None, "pre"),
        P("pre", "head"),
        P("pre", "head"),
        P("pre", "head"),
    )
    out_specs = P(("grp", "pre"), None, "head")
    return jax.shard_map(
        on_device, mesh=mesh, in_specs=in_specs, out_specs=out_specs, check_vma=False
    )
```
